512 devices in a mesh: ctx: 128 (over z_hi, y, x), head: 4 (over z_lo, core).
Axes of the slice: x: 4, y: 8, z: 8 (z_hi: 4, z_lo: 2; z = z_hi * 2 + z_lo), core: 2. Of those that a mesh axis runs over, the one named last changes fastest.
Arguments:
- queries: bfloat16 [65536, 4096], P(('ctx', 'head')), may hold values from -8 to 8
- keys: bfloat16 [65536, 512], P(('ctx', 'head')), may hold values from -8 to 8
- values: bfloat16 [65536, 512], P(('ctx', 'head')), may hold values from -6 to 6
- doc_lengths: int32 [256], replicated, may hold values from 1 to 2048, 65536 in all
Outputs:
- attended: bfloat16 [65536, 4096], P('ctx', 'head')
The draws below stay inside these ranges and needn't reach their ends.
Inputs may be any that keep to these rules, and one draw needn't show every extreme that they name: `doc_lengths`: the lengths sum to 65536 and the largest is exactly 2048.
All inputs are finite; a program needn't handle non-finite values.
Results may differ from the reference program's by a relative error of at most 0.012.
Values may be sent and summed in bfloat16 or wider, within the bound.
A program may use at most 64 MiB of HBM per device.

```python
import math
import jax
import jax.numpy as jnp
import numpy as np
from jax import lax

QUERY_HEADS = 32
KEY_VALUE_HEADS = 4
HEAD_SIZE = 128
SPAN = 4
TOK_CTX = 512
PACKED_TOKENS = 65536
MOST = 2048
NDOCS = 256
N_CTX = 128


def draw_queries(key, part):
    key = jax.random.fold_in(key, 11)
    drawn_sample = jnp.clip(jax.random.normal(key, (PACKED_TOKENS, QUERY_HEADS, HEAD_SIZE), jnp.float32), -8.0, 8.0)
    return drawn_sample.reshape(PACKED_TOKENS, QUERY_HEADS * HEAD_SIZE).astype(jnp.bfloat16)


def draw_keys(key, part):
    key = jax.random.fold_in(key, 12)
    drawn_sample = jnp.clip(jax.random.normal(key, (PACKED_TOKENS, KEY_VALUE_HEADS, HEAD_SIZE), jnp.float32), -8.0, 8.0)
    return drawn_sample.reshape(PACKED_TOKENS, KEY_VALUE_HEADS * HEAD_SIZE).astype(jnp.bfloat16)


def shard_levels(stream_key, extent, cuts, low, largest):
    def one(axis_at, blocks):
        steps = jax.random.uniform(jax.random.fold_in(jax.random.fold_in(stream_key, 6), axis_at), (blocks,), jnp.float32, low / len(cuts), largest / len(cuts))
        return jnp.repeat(jnp.exp(steps), extent[axis_at] // blocks).reshape((-1,) + (1,) * (len(extent) - axis_at - 1))

    gain = one(*cuts[0])
    for cut in cuts[1:]:
        gain = gain * one(*cut)
    return gain


def length_profile(amount, total, most, skew):
    loads = [(1 << 20) // math.isqrt(rank ** skew) + 1 for rank in range(2, amount + 1)]
    rest, holding = total - most - (amount - 1), [1] * (amount - 1)
    while rest > 0:
        movable = [i for i in range(amount - 1) if holding[i] < most]
        pool, left = sum([loads[i] for i in movable]), rest
        for i in movable:
            more = min(most - holding[i], max(1, left * loads[i] // pool), rest)
            holding[i] = holding[i] + more
            rest = rest - more
    return np.array([most] + holding)


def ragged(stream_key, number_of, total, reach, slope):
    if number_of == 2:
        one = jax.random.randint(stream_key, (), max(1, total - reach), min(reach, total - 1) + 1)
        return jnp.stack([one, total - one])
    lengths = jnp.asarray(length_profile(number_of, total, reach, slope), jnp.int32)
    couples = (number_of - 1) // 2
    donor, receiver = lengths[1:1 + 2 * couples:2], lengths[2:2 + 2 * couples:2]
    margin = jnp.minimum(donor - 1, reach - receiver)
    passed = jax.random.randint(jax.random.fold_in(stream_key, 1), (couples,), 0, 1 << 20) % (margin + 1)
    lengths = lengths.at[1:1 + 2 * couples:2].set(donor - passed).at[2:2 + 2 * couples:2].set(receiver + passed)
    return lengths[jax.random.permutation(jax.random.fold_in(stream_key, 2), number_of)]


def normal_values(rng, dims, width, bound, cuts=(), kind=jnp.bfloat16):
    result = width * jax.random.normal(rng, dims, jnp.float32)
    if cuts:
        result = result * shard_levels(rng, dims, cuts, -0.22, 0.18)
    return jnp.clip(result, -bound, bound).astype(kind)


def setup_inputs(seed: int = 0) -> dict:
    splits = jax.random.split(jax.random.key(seed), 5)
    return {
        "queries": draw_queries(jax.random.fold_in(splits[4], 71), 0),
        "keys": draw_keys(jax.random.fold_in(splits[4], 71), 0),
        "values": normal_values(splits[2], (PACKED_TOKENS, KEY_VALUE_HEADS * HEAD_SIZE), 1.0, 6.0, ((0, 512),)),
        "doc_lengths": ragged(splits[3], NDOCS, PACKED_TOKENS, MOST, 2).astype(jnp.int32),
    }


lowest_score = -1e+30

def segment_of(positions, doc_ends):
    return lax.optimization_barrier(jnp.sum((positions[:, None] >= doc_ends[None, :]).astype(jnp.int32), axis=1)).astype(jnp.int32)

def reference(queries, keys, values, doc_lengths):
    shared_heads = QUERY_HEADS // KEY_VALUE_HEADS
    leading_part = SPAN * TOK_CTX
    window = (SPAN + 1) * TOK_CTX
    score_scale = 1.0 / math.sqrt(HEAD_SIZE)
    doc_ends = jnp.cumsum(doc_lengths).astype(jnp.int32)
    heads_of_query = queries.reshape(PACKED_TOKENS, KEY_VALUE_HEADS, shared_heads, HEAD_SIZE)
    padded_keys = jnp.concatenate([jnp.zeros((leading_part, KEY_VALUE_HEADS, HEAD_SIZE), jnp.bfloat16), keys.reshape(PACKED_TOKENS, KEY_VALUE_HEADS, HEAD_SIZE)], axis=0)
    padded_values = jnp.concatenate([jnp.zeros((leading_part, KEY_VALUE_HEADS, HEAD_SIZE), jnp.bfloat16), values.reshape(PACKED_TOKENS, KEY_VALUE_HEADS, HEAD_SIZE)], axis=0)
    positions = jnp.arange(PACKED_TOKENS, dtype=jnp.int32)
    segments = segment_of(positions, doc_ends)
    pos_padded = jnp.concatenate([jnp.arange(leading_part, dtype=jnp.int32) - leading_part, positions])
    seg_padded = jnp.concatenate([jnp.full((leading_part,), -1, jnp.int32), segments])

    def one_block(block_index):
        first = (block_index * TOK_CTX).astype(jnp.int32)
        query_block = lax.dynamic_slice_in_dim(heads_of_query, first, TOK_CTX, 0)
        key_block = lax.dynamic_slice_in_dim(padded_keys, first, window, 0)
        value_block = lax.dynamic_slice_in_dim(padded_values, first, window, 0)
        query_pos = lax.dynamic_slice_in_dim(positions, first, TOK_CTX, 0)
        query_seg = lax.dynamic_slice_in_dim(segments, first, TOK_CTX, 0)
        key_pos = lax.dynamic_slice_in_dim(pos_padded, first, window, 0)
        key_seg = lax.dynamic_slice_in_dim(seg_padded, first, window, 0)
        scores = jnp.einsum('qhgd,khd->hgqk', query_block.astype(jnp.float32), key_block.astype(jnp.float32)) * score_scale
        allowed = (key_seg[None, :] == query_seg[:, None]) & (key_pos[None, :] <= query_pos[:, None]) & (key_pos[None, :] >= 0)
        scores = jnp.where(allowed, scores, lowest_score)
        highest = lax.optimization_barrier(jnp.max(scores, axis=-1, keepdims=True))
        weights = jnp.where(allowed, jnp.exp(scores - highest), 0.0)
        totals = lax.optimization_barrier(jnp.sum(weights, axis=-1))
        rounded = lax.optimization_barrier(weights.astype(jnp.bfloat16))
        summed = jnp.einsum('hgqk,khd->qhgd', rounded.astype(jnp.float32), value_block.astype(jnp.float32))
        divided = summed / jnp.transpose(totals, (2, 0, 1))[..., None]
        return divided.reshape(TOK_CTX, QUERY_HEADS * HEAD_SIZE).astype(jnp.bfloat16)
    blocks_out = lax.map(one_block, jnp.arange(N_CTX, dtype=jnp.int32))
    return blocks_out.reshape(PACKED_TOKENS, QUERY_HEADS * HEAD_SIZE)
```

```python
import functools
import math

import jax
import jax.numpy as jnp
from jax import lax
from jax.experimental import pallas as pl
from jax.experimental.pallas import tpu as pltpu
from jax.sharding import PartitionSpec as P

QUERY_HEADS = 32
KEY_VALUE_HEADS = 4
HEAD_SIZE = 128
SPAN = 4
BLOCK = 512
CHUNK = 128
BACK = SPAN * BLOCK
WINDOW = BACK + BLOCK
PACKED = 65536
HEADS = QUERY_HEADS // KEY_VALUE_HEADS
SCALE = math.log2(math.e) / math.sqrt(HEAD_SIZE)
APART = -32768.0

MESH = pl.DeviceIdType.MESH
F32 = jnp.float32
BF16 = jnp.bfloat16

STACK = 4
QROWS = 128
BAND = BACK + QROWS
TILES = [(s, min(512, BAND - s)) for s in range(0, BAND, 512)]


def nt(a, b):
    return lax.dot_general(a, b, (((1,), (1,)), ((), ())), preferred_element_type=F32)


def nn(a, b):
    return lax.dot_general(a, b, (((1,), (0,)), ((), ())), preferred_element_type=F32)


def partners(head):
    return [head, head + 1 - 2 * (head % 2), (head + 2) % 4, 3 - head]


def mark_documents(group, len_ref, kf, qf):
    lens = jnp.broadcast_to(len_ref[...], (16, 256))
    upto = (
        lax.broadcasted_iota(jnp.int32, (256, 256), 0)
        <= lax.broadcasted_iota(jnp.int32, (256, 256), 1)
    ).astype(F32).astype(BF16)
    high = (lens // 16).astype(F32).astype(BF16)
    low = (lens % 16).astype(F32).astype(BF16)
    ends = (nn(high, upto) * 16.0 + nn(low, upto))[0:1, :].astype(jnp.int32)
    ones = jnp.ones((256, 128), BF16)
    lane = lax.broadcasted_iota(jnp.int32, (512, 128), 1)
    for d in range(SPAN + 1):
        base = d * BLOCK
        pos = lax.broadcasted_iota(jnp.int32, (512, 256), 0) + (group * BLOCK + base + (PACKED - BACK)) % PACKED
        passed = jnp.where(ends <= pos, 1.0, 0.0).astype(BF16)
        index = nn(passed, ones).astype(jnp.int32)
        bit = jnp.right_shift(index, lane // 2) & 1
        differs = jnp.where(lane % 2 == 0, 1 - bit, bit)
        inside = lane < 16
        kf[base : base + BLOCK, :] = jnp.where(inside, differs.astype(F32) * APART, 0.0).astype(BF16)
        if d == SPAN:
            qf[...] = jnp.where(inside, (1 - differs).astype(F32), 0.0).astype(BF16)


def scores_into(item_heads, qt, buf, qbuf, kv, kf, qf):
    rows = slice(qt * QROWS, (qt + 1) * QROWS)
    marks = qf[rows, :]
    q = jnp.concatenate(
        [jnp.concatenate([qbuf[h, rows, :], marks], axis=1) for h in item_heads], axis=0
    )
    causal = lax.broadcasted_iota(jnp.int32, (QROWS, QROWS), 1) <= lax.broadcasted_iota(
        jnp.int32, (QROWS, QROWS), 0
    )
    causal = jnp.concatenate([causal] * STACK, axis=0)
    top = None
    for s, n in TILES:
        lo = qt * QROWS + s
        k = jnp.concatenate([kv[0, lo : lo + n, :], kf[lo : lo + n, :]], axis=1)
        sc = nt(q, k)
        if s + n == BAND:
            last = jnp.where(causal, sc[:, n - QROWS :], -1e30)
            sc = jnp.concatenate([sc[:, : n - QROWS], last], axis=1) if n > QROWS else last
        buf[:, s : s + n] = sc
        for a in range(0, n, 128):
            part = sc[:, a : a + 128]
            top = part if top is None else jnp.maximum(top, part)
    return jnp.max(top, axis=1, keepdims=True) * SCALE


def weigh(qt, buf, top, kv):
    acc = None
    for s, n in TILES:
        lo = qt * QROWS + s
        p = jnp.exp2(buf[:, s : s + n] * SCALE - top).astype(BF16)
        v = jnp.concatenate([kv[1, lo : lo + n, :], jnp.ones((n, 128), BF16)], axis=1)
        part = nn(p, v)
        acc = part if acc is None else acc + part
    return (acc[:, :128] / acc[:, 128:]).astype(BF16)


def kernel(
    len_ref, q_ref, k_ref, v_ref, o_ref,
    qbuf, kv, kf, qf, out, s0, s1,
    kv_send, kv_recv, q_send, q_recv, c_send, c_recv, o_sem,
):
    group = lax.axis_index("ctx")
    head = lax.axis_index("head")
    x = group % 4
    row = group // 4
    below = (group + 4) % 128
    above = (group + 124) % 128
    mates = partners(head)
    across = [row * 4 + (x + d) % 4 for d in range(4)]

    barrier = pltpu.get_barrier_semaphore()
    greet = [(group, m) for m in mates[1:]]
    greet += [(c, head) for c in across[1:]] + [(below, head), (above, head)]
    for who in greet:
        pl.semaphore_signal(barrier, inc=1, device_id=who, device_id_type=MESH)
    pl.semaphore_wait(barrier, len(greet))

    own = pl.ds(pl.multiple_of(head * CHUNK, CHUNK), CHUNK)
    own_kv = pl.ds(pl.multiple_of(BACK + head * CHUNK, CHUNK), CHUNK)

    def columns(start):
        return pl.ds(pl.multiple_of(start, 128), 128)

    def kv_copy(which, i):
        src = (k_ref, v_ref)[which].at[:, columns(mates[i] * 128)]
        dst = kv.at[which, own_kv, :]
        if i == 0:
            return pltpu.make_async_copy(src, dst, kv_recv.at[which, 0])
        return pltpu.make_async_remote_copy(
            src_ref=src, dst_ref=dst, send_sem=kv_send.at[which, i], recv_sem=kv_recv.at[which, i],
            device_id=(group, mates[i]), device_id_type=MESH,
        )

    def q_copy(j, i):
        src = q_ref.at[:, columns((mates[i] * HEADS + j) * 128)]
        dst = qbuf.at[j, own, :]
        if i == 0:
            return pltpu.make_async_copy(src, dst, q_recv.at[j, 0])
        return pltpu.make_async_remote_copy(
            src_ref=src, dst_ref=dst, send_sem=q_send.at[j, i], recv_sem=q_recv.at[j, i],
            device_id=(group, mates[i]), device_id_type=MESH,
        )

    def chunk(slot, i):
        return pl.ds(pl.multiple_of(slot * BLOCK + mates[i] * CHUNK, CHUNK), CHUNK)

    def ctx_copy(d, i, source):
        return pltpu.make_async_remote_copy(
            src_ref=kv.at[:, chunk(source, i), :], dst_ref=kv.at[:, chunk(SPAN - d, i), :],
            send_sem=c_send.at[d - 1, i], recv_sem=c_recv.at[d - 1, i],
            device_id=(below if d == 4 else across[d], head), device_id_type=MESH,
        )

    order = (2, 3, 1, 0)
    for i in order:
        for which in range(2):
            kv_copy(which, i).start()
    for j in range(HEADS):
        for i in order:
            q_copy(j, i).start()

    mark_documents(group, len_ref, kf, qf)

    for i in range(4):
        for which in range(2):
            if i == 0:
                kv_copy(which, i).wait()
            else:
                kv_copy(which, i).wait_recv()
        ctx_copy(4, i, SPAN).start()
        for d in (1, 3, 2):
            @pl.when(x + d < 4)
            def _(d=d, i=i):
                ctx_copy(d, i, SPAN).start()
    for i in range(4):
        ctx_copy(4, i, SPAN).wait_recv()
        for d in (1, 3, 2):
            @pl.when(x + d >= 4)
            def _(d=d, i=i):
                ctx_copy(d, i, 0).start()
    for d in (1, 3, 2):
        for i in range(4):
            ctx_copy(d, i, SPAN).wait_recv()
    for j in range(HEADS):
        for i in range(4):
            if i == 0:
                q_copy(j, i).wait()
            else:
                q_copy(j, i).wait_recv()

    bufs = (s0, s1)
    tiles_q = BLOCK // QROWS
    groups = HEADS // STACK

    def item_heads(jb):
        return [jb * STACK + h for h in range(STACK)]

    def out_copy(jb, qt):
        part = (pl.ds(qt * QROWS, QROWS), pl.ds(pl.multiple_of(jb * STACK * 128, 128), STACK * 128))
        return pltpu.make_async_copy(out.at[part], o_ref.at[part], o_sem.at[jb, qt])

    first = scores_into(item_heads(0), 0, s0, qbuf, kv, kf, qf)

    def body(jb, top):
        for qt in range(tiles_q):
            next_jb = jnp.minimum(jb + (qt + 1) // tiles_q, groups - 1)
            later = scores_into(item_heads(next_jb), (qt + 1) % tiles_q, bufs[(qt + 1) % 2], qbuf, kv, kf, qf)
            result = weigh(qt, bufs[qt % 2], top, kv)
            for h in range(STACK):
                out[qt * QROWS : (qt + 1) * QROWS, columns((jb * STACK + h) * 128)] = result[
                    h * QROWS : (h + 1) * QROWS
                ]
            out_copy(jb, qt).start()
            top = later
        return top

    lax.fori_loop(0, groups, body, first)

    for i in range(1, 4):
        for which in range(2):
            kv_copy(which, i).wait_send()
        for j in range(HEADS):
            q_copy(j, i).wait_send()
    for d in range(1, SPAN + 1):
        for i in range(4):
            ctx_copy(d, i, SPAN).wait_send()
    for jb in range(groups):
        for qt in range(tiles_q):
            out_copy(jb, qt).wait()


def shards(queries, keys, values, doc_lengths):
    anywhere = pl.BlockSpec(memory_space=pl.ANY)
    return pl.pallas_call(
        kernel,
        out_shape=jax.ShapeDtypeStruct((BLOCK, HEADS * HEAD_SIZE), BF16),
        in_specs=[pl.BlockSpec(memory_space=pltpu.VMEM), anywhere, anywhere, anywhere],
        out_specs=anywhere,
        scratch_shapes=[
            pltpu.VMEM((HEADS, BLOCK, HEAD_SIZE), BF16),
            pltpu.VMEM((2, WINDOW, HEAD_SIZE), BF16),
            pltpu.VMEM((WINDOW, HEAD_SIZE), BF16),
            pltpu.VMEM((BLOCK, HEAD_SIZE), BF16),
            pltpu.VMEM((BLOCK, HEADS * HEAD_SIZE), BF16),
            pltpu.VMEM((STACK * QROWS, BAND), F32),
            pltpu.VMEM((STACK * QROWS, BAND), F32),
            pltpu.SemaphoreType.DMA((2, 4)),
            pltpu.SemaphoreType.DMA((2, 4)),
            pltpu.SemaphoreType.DMA((HEADS, 4)),
            pltpu.SemaphoreType.DMA((HEADS, 4)),
            pltpu.SemaphoreType.DMA((SPAN, 4)),
            pltpu.SemaphoreType.DMA((SPAN, 4)),
            pltpu.SemaphoreType.DMA((HEADS // STACK, BLOCK // QROWS)),
        ],
        compiler_params=pltpu.CompilerParams(
            collective_id=0, has_side_effects=True, vmem_limit_bytes=56 * 2**20
        ),
    )(doc_lengths.reshape(1, -1), queries, keys, values)


def solution(mesh):
    placed = (P(("ctx", "head"), None), P(("ctx", "head"), None), P(("ctx", "head"), None), P())
    return jax.shard_map(
        shards, mesh=mesh, in_specs=placed, out_specs=P("ctx", "head"), check_vma=False
    )
```

```python
import functools
import math

import jax
import jax.numpy as jnp
from jax import lax
from jax.experimental import pallas as pl
from jax.experimental.pallas import tpu as pltpu
from jax.sharding import PartitionSpec as P

QUERY_HEADS = 32
KEY_VALUE_HEADS = 4
HEAD_SIZE = 128
SPAN = 4
BLOCK = 512
CHUNK = 128
BACK = SPAN * BLOCK
WINDOW = BACK + BLOCK
PACKED = 65536
HEADS = QUERY_HEADS // KEY_VALUE_HEADS
SCALE = math.log2(math.e) / math.sqrt(HEAD_SIZE)
APART = -32768.0

MESH = pl.DeviceIdType.MESH
F32 = jnp.float32
BF16 = jnp.bfloat16

STACK = 4
QROWS = 128
BAND = BACK + QROWS


def nt(a, b):
    return lax.dot_general(a, b, (((1,), (1,)), ((), ())), preferred_element_type=F32)


def nn(a, b):
    return lax.dot_general(a, b, (((1,), (0,)), ((), ())), preferred_element_type=F32)


def partners(head):
    return [head, head + 1 - 2 * (head % 2), (head + 2) % 4, 3 - head]


def mark_documents(group, len_ref, kf, qf):
    lens = jnp.broadcast_to(len_ref[...], (16, 256))
    upto = (
        lax.broadcasted_iota(jnp.int32, (256, 256), 0)
        <= lax.broadcasted_iota(jnp.int32, (256, 256), 1)
    ).astype(F32).astype(BF16)
    high = (lens // 16).astype(F32).astype(BF16)
    low = (lens % 16).astype(F32).astype(BF16)
    ends = (nn(high, upto) * 16.0 + nn(low, upto))[0:1, :].astype(jnp.int32)
    ones = jnp.ones((256, 128), BF16)
    lane = lax.broadcasted_iota(jnp.int32, (512, 128), 1)
    for d in range(SPAN + 1):
        base = d * BLOCK
        pos = lax.broadcasted_iota(jnp.int32, (512, 256), 0) + (group * BLOCK + base + (PACKED - BACK)) % PACKED
        passed = jnp.where(ends <= pos, 1.0, 0.0).astype(BF16)
        index = nn(passed, ones).astype(jnp.int32)
        bit = jnp.right_shift(index, lane // 2) & 1
        differs = jnp.where(lane % 2 == 0, 1 - bit, bit)
        inside = lane < 16
        kf[base : base + BLOCK, :] = jnp.where(inside, differs.astype(F32) * APART, 0.0).astype(BF16)
        if d == SPAN:
            qf[...] = jnp.where(inside, (1 - differs).astype(F32), 0.0).astype(BF16)


def pieces(qt):
    reach = [(qt * QROWS, BLOCK - qt * QROWS), (BLOCK, BLOCK), (3 * BLOCK, BLOCK)]
    return reach + [(BACK, (qt + 1) * QROWS)]


def score(q, spans, buf, kv, kf, causal):
    at, top = 0, None
    for lo, n in spans:
        k = jnp.concatenate([kv[0, lo : lo + n, :], kf[lo : lo + n, :]], axis=1)
        sc = nt(q, k)
        if lo == BACK:
            last = jnp.where(causal, sc[:, n - QROWS :], -1e30)
            sc = jnp.concatenate([sc[:, : n - QROWS], last], axis=1) if n > QROWS else last
        buf[:, at : at + n] = sc
        for a in range(0, n, 128):
            part = sc[:, a : a + 128]
            top = part if top is None else jnp.maximum(top, part)
        at += n
    return jnp.broadcast_to(jnp.max(top, axis=1, keepdims=True) * SCALE, top.shape)


def weigh(spans, buf, top, kv):
    at, acc = 0, None
    for lo, n in spans:
        shift = jnp.concatenate([top] * (n // 128), axis=1)
        p = jnp.exp2(buf[:, at : at + n] * SCALE - shift).astype(BF16)
        v = jnp.concatenate([kv[1, lo : lo + n, :], jnp.ones((n, 128), BF16)], axis=1)
        part = nn(p, v)
        acc = part if acc is None else acc + part
        at += n
    return acc


def kernel(
    len_ref, q_ref, k_ref, v_ref, o_ref,
    qbuf, kv, kf, qf, out, s0, s1, accs, tops,
    kv_send, kv_recv, q_send, q_recv, c_send, c_recv, raw_send, o_sem,
):
    group = lax.axis_index("ctx")
    head = lax.axis_index("head")
    x = group % 4
    row = group // 4
    below = (group + 4) % 128
    above = (group + 124) % 128
    right = row * 4 + (x + 1) % 4
    left = row * 4 + (x + 3) % 4
    pair = group + 1 - 2 * (x % 2)
    mates = partners(head)
    has_above = row > 0
    has_below = row < 31
    crosses = jnp.logical_and(row % 8 == 7, has_below)
    crossed = jnp.logical_and(row % 8 == 0, has_above)
    lower = head < 2

    barrier = pltpu.get_barrier_semaphore()

    def greet(who):
        pl.semaphore_signal(barrier, inc=1, device_id=who, device_id_type=MESH)

    for m in mates[1:]:
        greet((group, m))
    greet((right, head))
    greet((left, head))

    @pl.when(has_below)
    def _():
        greet((below, head))

    @pl.when(has_above)
    def _():
        greet((above, head))

    raw_out = jnp.logical_and(crosses, jnp.logical_not(lower))
    raw_in = jnp.logical_and(crossed, lower)

    @pl.when(raw_out)
    def _():
        greet((below, mates[2]))
        greet((below, mates[3]))

    @pl.when(raw_in)
    def _():
        greet((above, mates[2]))
        greet((above, mates[3]))

    greeters = 5 + has_below.astype(jnp.int32) + has_above.astype(jnp.int32)
    pl.semaphore_wait(barrier, greeters + 2 * jnp.logical_or(raw_out, raw_in).astype(jnp.int32))

    own = pl.ds(pl.multiple_of(head * CHUNK, CHUNK), CHUNK)
    own_kv = pl.ds(pl.multiple_of(BACK + head * CHUNK, CHUNK), CHUNK)

    def columns(start):
        return pl.ds(pl.multiple_of(start, 128), 128)

    def kv_copy(which, i):
        src = (k_ref, v_ref)[which].at[:, columns(mates[i] * 128)]
        dst = kv.at[which, own_kv, :]
        if i == 0:
            return pltpu.make_async_copy(src, dst, kv_recv.at[which, 0])
        return pltpu.make_async_remote_copy(
            src_ref=src, dst_ref=dst, send_sem=kv_send.at[which, i], recv_sem=kv_recv.at[which, i],
            device_id=(group, mates[i]), device_id_type=MESH,
        )

    def q_copy(j, i):
        src = q_ref.at[:, columns((mates[i] * HEADS + j) * 128)]
        dst = qbuf.at[j, own, :]
        if i == 0:
            return pltpu.make_async_copy(src, dst, q_recv.at[j, 0])
        return pltpu.make_async_remote_copy(
            src_ref=src, dst_ref=dst, send_sem=q_send.at[j, i], recv_sem=q_recv.at[j, i],
            device_id=(group, mates[i]), device_id_type=MESH,
        )

    def chunk(slot, i):
        return pl.ds(pl.multiple_of(slot * BLOCK + mates[i] * CHUNK, CHUNK), CHUNK)

    def ctx_copy(d, i, source):
        target = {1: right, 2: pair, 3: left, 4: below}[d]
        return pltpu.make_async_remote_copy(
            src_ref=kv.at[:, chunk(source, i), :], dst_ref=kv.at[:, chunk(SPAN - d, i), :],
            send_sem=c_send.at[d - 1, i], recv_sem=c_recv.at[d - 1, i],
            device_id=(target, head), device_id_type=MESH,
        )

    def raw_copy(which, i):
        src = (k_ref, v_ref)[which].at[:, columns(mates[i] * 128)]
        return pltpu.make_async_remote_copy(
            src_ref=src, dst_ref=kv.at[which, own, :],
            send_sem=raw_send.at[which, i - 2], recv_sem=c_recv.at[3, i],
            device_id=(below, mates[i]), device_id_type=MESH,
        )

    order = (2, 3, 1, 0)
    for i in order:
        for which in range(2):
            kv_copy(which, i).start()

    @pl.when(raw_out)
    def _():
        for i in (2, 3):
            for which in range(2):
                raw_copy(which, i).start()

    for j in range(HEADS):
        for i in order:
            q_copy(j, i).start()

    for d in range(1, SPAN + 1):
        @pl.when(group < d)
        def _(d=d):
            kv[:, (SPAN - d) * BLOCK : (SPAN - d + 1) * BLOCK, :] = jnp.zeros((2, BLOCK, HEAD_SIZE), BF16)

    mark_documents(group, len_ref, kf, qf)

    def sends_below(i):
        if i < 2:
            return has_below
        return jnp.logical_and(has_below, jnp.logical_not(jnp.logical_and(crosses, lower)))

    def takes(d):
        return group >= d

    own_right = x < 3
    own_left = x == 0
    up_right = jnp.logical_and(x == 3, has_above)
    up_left = jnp.logical_and(x > 0, has_above)
    sends_right = jnp.logical_or(own_right, up_right)
    sends_left = jnp.logical_or(own_left, up_left)
    sends_pair = jnp.logical_or(x >= 2, has_above)
    even = x % 2 == 0

    def stage_own(i):
        for which in range(2):
            if i == 0:
                kv_copy(which, i).wait()
            else:
                kv_copy(which, i).wait_recv()

        @pl.when(sends_below(i))
        def _():
            ctx_copy(4, i, SPAN).start()

        @pl.when(own_right)
        def _():
            ctx_copy(1, i, SPAN).start()

        @pl.when(own_left)
        def _():
            ctx_copy(3, i, SPAN).start()

    def stage_up(i):
        @pl.when(has_above)
        def _():
            ctx_copy(4, i, SPAN).wait_recv()

        @pl.when(up_right)
        def _():
            ctx_copy(1, i, 0).start()

        @pl.when(up_left)
        def _():
            ctx_copy(3, i, 0).start()

    def stage_pair(i):
        @pl.when(takes(1))
        def _():
            ctx_copy(1, i, SPAN).wait_recv()

        @pl.when(takes(3))
        def _():
            ctx_copy(3, i, SPAN).wait_recv()

        @pl.when(jnp.logical_and(sends_pair, even))
        def _():
            ctx_copy(2, i, SPAN - 1).start()

        @pl.when(jnp.logical_and(sends_pair, jnp.logical_not(even)))
        def _():
            ctx_copy(2, i, SPAN - 3).start()

    for i in range(4):
        stage_own(i)
    stage_up(0)
    stage_up(1)
    stage_pair(0)
    stage_up(2)
    stage_pair(1)
    stage_up(3)
    stage_pair(2)
    stage_pair(3)

    bufs = (s0, s1)
    tiles_q = BLOCK // QROWS
    groups = HEADS // STACK
    causal = lax.broadcasted_iota(jnp.int32, (QROWS, QROWS), 1) <= lax.broadcasted_iota(
        jnp.int32, (QROWS, QROWS), 0
    )
    causal = jnp.concatenate([causal] * STACK, axis=0)
    two_back = [(2 * BLOCK, BLOCK)]

    def rows_of(jb, qt):
        rows = slice(qt * QROWS, (qt + 1) * QROWS)
        marks = qf[rows, :]
        return jnp.concatenate(
            [jnp.concatenate([qbuf[jb * STACK + h, rows, :], marks], axis=1) for h in range(STACK)], axis=0
        )

    def out_copy(jb, qt):
        part = (pl.ds(qt * QROWS, QROWS), pl.ds(pl.multiple_of(jb * STACK * 128, 128), STACK * 128))
        return pltpu.make_async_copy(out.at[part], o_ref.at[part], o_sem.at[jb, qt])

    def early(jb, _):
        for h in range(STACK):
            for i in range(4):
                if i == 0:
                    q_copy(jb * STACK + h, i).wait()
                else:
                    q_copy(jb * STACK + h, i).wait_recv()

        def finish(qt, top):
            accs[jb, qt] = weigh(pieces(qt), bufs[qt % 2], top, kv)
            tops[jb, qt] = top

        before = None
        for qt in range(tiles_q):
            top = score(rows_of(jb, qt), pieces(qt), bufs[qt % 2], kv, kf, causal)
            if qt:
                finish(qt - 1, before)
            before = top
        finish(tiles_q - 1, before)
        return 0

    lax.fori_loop(0, groups, early, 0)

    for i in range(4):
        @pl.when(takes(2))
        def _(i=i):
            ctx_copy(2, i, SPAN).wait_recv()

    def late(jb, _):
        def finish(qt, top):
            earlier = tops[jb, qt]
            both = jnp.maximum(earlier, top)
            factor = jnp.exp2(earlier - both)
            acc = accs[jb, qt] * jnp.concatenate([factor, factor], axis=1)
            acc = acc + weigh(two_back, bufs[qt % 2], both, kv)
            result = (acc[:, :128] / acc[:, 128:]).astype(BF16)
            for h in range(STACK):
                out[qt * QROWS : (qt + 1) * QROWS, columns((jb * STACK + h) * 128)] = result[
                    h * QROWS : (h + 1) * QROWS
                ]
            out_copy(jb, qt).start()

        before = None
        for qt in range(tiles_q):
            top = score(rows_of(jb, qt), two_back, bufs[qt % 2], kv, kf, causal)
            if qt:
                finish(qt - 1, before)
            before = top
        finish(tiles_q - 1, before)
        return 0

    lax.fori_loop(0, groups, late, 0)

    for i in range(1, 4):
        for which in range(2):
            kv_copy(which, i).wait_send()
        for j in range(HEADS):
            q_copy(j, i).wait_send()

    @pl.when(raw_out)
    def _():
        for i in (2, 3):
            for which in range(2):
                raw_copy(which, i).wait_send()

    for i in range(4):
        for d, sends in ((1, sends_right), (2, sends_pair), (3, sends_left), (4, sends_below(i))):
            @pl.when(sends)
            def _(d=d, i=i):
                ctx_copy(d, i, SPAN).wait_send()
    for jb in range(groups):
        for qt in range(tiles_q):
            out_copy(jb, qt).wait()


def shards(queries, keys, values, doc_lengths):
    anywhere = pl.BlockSpec(memory_space=pl.ANY)
    stacked = STACK * QROWS
    items = (HEADS // STACK, BLOCK // QROWS)
    return pl.pallas_call(
        kernel,
        out_shape=jax.ShapeDtypeStruct((BLOCK, HEADS * HEAD_SIZE), BF16),
        in_specs=[pl.BlockSpec(memory_space=pltpu.VMEM), anywhere, anywhere, anywhere],
        out_specs=anywhere,
        scratch_shapes=[
            pltpu.VMEM((HEADS, BLOCK, HEAD_SIZE), BF16),
            pltpu.VMEM((2, WINDOW, HEAD_SIZE), BF16),
            pltpu.VMEM((WINDOW, HEAD_SIZE), BF16),
            pltpu.VMEM((BLOCK, HEAD_SIZE), BF16),
            pltpu.VMEM((BLOCK, HEADS * HEAD_SIZE), BF16),
            pltpu.VMEM((stacked, BAND - BLOCK), F32),
            pltpu.VMEM((stacked, BAND - BLOCK), F32),
            pltpu.VMEM((*items, stacked, 2 * HEAD_SIZE), F32),
            pltpu.VMEM((*items, stacked, HEAD_SIZE), F32),
            pltpu.SemaphoreType.DMA((2, 4)),
            pltpu.SemaphoreType.DMA((2, 4)),
            pltpu.SemaphoreType.DMA((HEADS, 4)),
            pltpu.SemaphoreType.DMA((HEADS, 4)),
            pltpu.SemaphoreType.DMA((SPAN, 4)),
            pltpu.SemaphoreType.DMA((SPAN, 4)),
            pltpu.SemaphoreType.DMA((2, 2)),
            pltpu.SemaphoreType.DMA(items),
        ],
        compiler_params=pltpu.CompilerParams(
            collective_id=0, has_side_effects=True, vmem_limit_bytes=56 * 2**20
        ),
    )(doc_lengths.reshape(1, -1), queries, keys, values)


def solution(mesh):
    placed = (P(("ctx", "head"), None), P(("ctx", "head"), None), P(("ctx", "head"), None), P())
    return jax.shard_map(
        shards, mesh=mesh, in_specs=placed, out_specs=P("ctx", "head"), check_vma=False
    )
```

```python
import functools
import math

import jax
import jax.numpy as jnp
from jax import lax
from jax.experimental import pallas as pl
from jax.experimental.pallas import tpu as pltpu
from jax.sharding import PartitionSpec as P

QUERY_HEADS = 32
KEY_VALUE_HEADS = 4
HEAD_SIZE = 128
SPAN = 4
BLOCK = 512
CHUNK = 128
BACK = SPAN * BLOCK
WINDOW = BACK + BLOCK
PACKED = 65536
HEADS = QUERY_HEADS // KEY_VALUE_HEADS
SCALE = math.log2(math.e) / math.sqrt(HEAD_SIZE)
APART = -32768.0

MESH = pl.DeviceIdType.MESH
F32 = jnp.float32
BF16 = jnp.bfloat16

STACK = 4
QROWS = 128
BAND = BACK + QROWS


def nt(a, b):
    return lax.dot_general(a, b, (((1,), (1,)), ((), ())), preferred_element_type=F32)


def nn(a, b):
    return lax.dot_general(a, b, (((1,), (0,)), ((), ())), preferred_element_type=F32)


def partners(head):
    return [head, head + 1 - 2 * (head % 2), (head + 2) % 4, 3 - head]


def mark_documents(group, len_ref, kf, qf):
    lens = jnp.broadcast_to(len_ref[...], (16, 256))
    upto = (
        lax.broadcasted_iota(jnp.int32, (256, 256), 0)
        <= lax.broadcasted_iota(jnp.int32, (256, 256), 1)
    ).astype(F32).astype(BF16)
    high = (lens // 16).astype(F32).astype(BF16)
    low = (lens % 16).astype(F32).astype(BF16)
    ends = (nn(high, upto) * 16.0 + nn(low, upto))[0:1, :].astype(jnp.int32)
    ones = jnp.ones((256, 128), BF16)
    lane = lax.broadcasted_iota(jnp.int32, (512, 128), 1)
    for d in range(SPAN + 1):
        base = d * BLOCK
        pos = lax.broadcasted_iota(jnp.int32, (512, 256), 0) + (group * BLOCK + base + (PACKED - BACK)) % PACKED
        passed = jnp.where(ends <= pos, 1.0, 0.0).astype(BF16)
        index = nn(passed, ones).astype(jnp.int32)
        bit = jnp.right_shift(index, lane // 2) & 1
        differs = jnp.where(lane % 2 == 0, 1 - bit, bit)
        inside = lane < 16
        kf[base : base + BLOCK, :] = jnp.where(inside, differs.astype(F32) * APART, 0.0).astype(BF16)
        if d == SPAN:
            qf[...] = jnp.where(inside, (1 - differs).astype(F32), 0.0).astype(BF16)


def near(qt):
    return [(BACK, (qt + 1) * QROWS), (qt * QROWS, BLOCK - qt * QROWS)]


MIDDLE = [(3 * BLOCK, BLOCK), (BLOCK, BLOCK)]
LAST = [(2 * BLOCK, BLOCK)]


def score(q, spans, buf, kv, kf, causal):
    at, top = 0, None
    for lo, n in spans:
        k = jnp.concatenate([kv[0, lo : lo + n, :], kf[lo : lo + n, :]], axis=1)
        sc = nt(q, k)
        if lo == BACK:
            last = jnp.where(causal, sc[:, n - QROWS :], -1e30)
            sc = jnp.concatenate([sc[:, : n - QROWS], last], axis=1) if n > QROWS else last
        buf[:, at : at + n] = sc
        for a in range(0, n, 128):
            part = sc[:, a : a + 128]
            top = part if top is None else jnp.maximum(top, part)
        at += n
    return jnp.broadcast_to(jnp.max(top, axis=1, keepdims=True) * SCALE, top.shape)


def weigh(spans, buf, top, kv):
    at, acc = 0, None
    for lo, n in spans:
        shift = jnp.concatenate([top] * (n // 128), axis=1)
        p = jnp.exp2(buf[:, at : at + n] * SCALE - shift).astype(BF16)
        v = jnp.concatenate([kv[1, lo : lo + n, :], jnp.ones((n, 128), BF16)], axis=1)
        part = nn(p, v)
        acc = part if acc is None else acc + part
        at += n
    return acc


def kernel(
    len_ref, q_ref, k_ref, v_ref, o_ref,
    qbuf, kv, kf, qf, out, s0, s1, accs, tops,
    kv_send, kv_recv, q_send, q_recv, c_send, c_recv, raw_send, o_sem,
):
    group = lax.axis_index("ctx")
    head = lax.axis_index("head")
    x = group % 4
    row = group // 4
    below = (group + 4) % 128
    above = (group + 124) % 128
    right = row * 4 + (x + 1) % 4
    left = row * 4 + (x + 3) % 4
    pair = group + 1 - 2 * (x % 2)
    mates = partners(head)
    has_above = row > 0
    has_below = row < 31
    crosses = jnp.logical_and(row % 8 == 7, has_below)
    crossed = jnp.logical_and(row % 8 == 0, has_above)
    lower = head < 2

    barrier = pltpu.get_barrier_semaphore()

    def greet(who):
        pl.semaphore_signal(barrier, inc=1, device_id=who, device_id_type=MESH)

    for m in mates[1:]:
        greet((group, m))
    greet((right, head))
    greet((left, head))

    @pl.when(has_below)
    def _():
        greet((below, head))

    @pl.when(has_above)
    def _():
        greet((above, head))

    raw_out = jnp.logical_and(crosses, jnp.logical_not(lower))
    raw_in = jnp.logical_and(crossed, lower)

    @pl.when(raw_out)
    def _():
        greet((below, mates[2]))
        greet((below, mates[3]))

    @pl.when(raw_in)
    def _():
        greet((above, mates[2]))
        greet((above, mates[3]))

    greeters = 5 + has_below.astype(jnp.int32) + has_above.astype(jnp.int32)
    pl.semaphore_wait(barrier, greeters + 2 * jnp.logical_or(raw_out, raw_in).astype(jnp.int32))

    own = pl.ds(pl.multiple_of(head * CHUNK, CHUNK), CHUNK)
    own_kv = pl.ds(pl.multiple_of(BACK + head * CHUNK, CHUNK), CHUNK)

    def columns(start):
        return pl.ds(pl.multiple_of(start, 128), 128)

    def kv_copy(which, i):
        src = (k_ref, v_ref)[which].at[:, columns(mates[i] * 128)]
        dst = kv.at[which, own_kv, :]
        if i == 0:
            return pltpu.make_async_copy(src, dst, kv_recv.at[which, 0])
        return pltpu.make_async_remote_copy(
            src_ref=src, dst_ref=dst, send_sem=kv_send.at[which, i], recv_sem=kv_recv.at[which, i],
            device_id=(group, mates[i]), device_id_type=MESH,
        )

    def q_copy(j, i):
        src = q_ref.at[:, columns((mates[i] * HEADS + j) * 128)]
        dst = qbuf.at[j, own, :]
        if i == 0:
            return pltpu.make_async_copy(src, dst, q_recv.at[j, 0])
        return pltpu.make_async_remote_copy(
            src_ref=src, dst_ref=dst, send_sem=q_send.at[j, i], recv_sem=q_recv.at[j, i],
            device_id=(group, mates[i]), device_id_type=MESH,
        )

    def chunk(slot, i):
        return pl.ds(pl.multiple_of(slot * BLOCK + mates[i] * CHUNK, CHUNK), CHUNK)

    def ctx_copy(d, i, source):
        target = {1: right, 2: pair, 3: left, 4: below}[d]
        return pltpu.make_async_remote_copy(
            src_ref=kv.at[:, chunk(source, i), :], dst_ref=kv.at[:, chunk(SPAN - d, i), :],
            send_sem=c_send.at[d - 1, i], recv_sem=c_recv.at[d - 1, i],
            device_id=(target, head), device_id_type=MESH,
        )

    def raw_copy(which, i):
        src = (k_ref, v_ref)[which].at[:, columns(mates[i] * 128)]
        return pltpu.make_async_remote_copy(
            src_ref=src, dst_ref=kv.at[which, own, :],
            send_sem=raw_send.at[which, i - 2], recv_sem=c_recv.at[3, i],
            device_id=(below, mates[i]), device_id_type=MESH,
        )

    order = (2, 3, 1, 0)
    for i in order:
        for which in range(2):
            kv_copy(which, i).start()

    @pl.when(raw_out)
    def _():
        for i in (2, 3):
            for which in range(2):
                raw_copy(which, i).start()

    for j in range(HEADS):
        for i in order:
            q_copy(j, i).start()

    for d in range(1, SPAN + 1):
        @pl.when(group < d)
        def _(d=d):
            kv[:, (SPAN - d) * BLOCK : (SPAN - d + 1) * BLOCK, :] = jnp.zeros((2, BLOCK, HEAD_SIZE), BF16)

    mark_documents(group, len_ref, kf, qf)

    def sends_below(i):
        if i < 2:
            return has_below
        return jnp.logical_and(has_below, jnp.logical_not(jnp.logical_and(crosses, lower)))

    def takes(d):
        return group >= d

    own_right = x < 3
    own_left = x == 0
    up_right = jnp.logical_and(x == 3, has_above)
    up_left = jnp.logical_and(x > 0, has_above)
    sends_right = jnp.logical_or(own_right, up_right)
    sends_left = jnp.logical_or(own_left, up_left)
    sends_pair = jnp.logical_or(x >= 2, has_above)
    even = x % 2 == 0

    def stage_own(i):
        for which in range(2):
            if i == 0:
                kv_copy(which, i).wait()
            else:
                kv_copy(which, i).wait_recv()

        @pl.when(sends_below(i))
        def _():
            ctx_copy(4, i, SPAN).start()

        @pl.when(own_right)
        def _():
            ctx_copy(1, i, SPAN).start()

        @pl.when(own_left)
        def _():
            ctx_copy(3, i, SPAN).start()

    def stage_up(i):
        @pl.when(has_above)
        def _():
            ctx_copy(4, i, SPAN).wait_recv()

        @pl.when(up_right)
        def _():
            ctx_copy(1, i, 0).start()

        @pl.when(up_left)
        def _():
            ctx_copy(3, i, 0).start()

    def stage_pair(i):
        @pl.when(takes(1))
        def _():
            ctx_copy(1, i, SPAN).wait_recv()

        @pl.when(takes(3))
        def _():
            ctx_copy(3, i, SPAN).wait_recv()

        @pl.when(jnp.logical_and(sends_pair, even))
        def _():
            ctx_copy(2, i, SPAN - 1).start()

        @pl.when(jnp.logical_and(sends_pair, jnp.logical_not(even)))
        def _():
            ctx_copy(2, i, SPAN - 3).start()

    stage_own(0)
    stage_own(1)

    @pl.when(jnp.logical_not(crossed))
    def _():
        stage_up(0)

    stage_own(2)
    stage_own(3)

    @pl.when(crossed)
    def _():
        stage_up(0)

    stage_up(1)
    stage_up(2)
    stage_pair(0)
    stage_up(3)
    stage_pair(1)

    bufs = (s0, s1)
    tiles_q = BLOCK // QROWS
    groups = HEADS // STACK
    causal = lax.broadcasted_iota(jnp.int32, (QROWS, QROWS), 1) <= lax.broadcasted_iota(
        jnp.int32, (QROWS, QROWS), 0
    )
    causal = jnp.concatenate([causal] * STACK, axis=0)

    def rows_of(jb, qt):
        rows = slice(qt * QROWS, (qt + 1) * QROWS)
        marks = qf[rows, :]
        return jnp.concatenate(
            [jnp.concatenate([qbuf[jb * STACK + h, rows, :], marks], axis=1) for h in range(STACK)], axis=0
        )

    def out_copy(jb, qt):
        part = (pl.ds(qt * QROWS, QROWS), pl.ds(pl.multiple_of(jb * STACK * 128, 128), STACK * 128))
        return pltpu.make_async_copy(out.at[part], o_ref.at[part], o_sem.at[jb, qt])

    def take_queries(jb):
        for h in range(STACK):
            for i in range(4):
                if i == 0:
                    q_copy(jb * STACK + h, i).wait()
                else:
                    q_copy(jb * STACK + h, i).wait_recv()

    def give(jb, qt, acc):
        result = (acc[:, :128] / acc[:, 128:]).astype(BF16)
        for h in range(STACK):
            out[qt * QROWS : (qt + 1) * QROWS, columns((jb * STACK + h) * 128)] = result[
                h * QROWS : (h + 1) * QROWS
            ]
        out_copy(jb, qt).start()

    def chain(items):
        pending = None
        for n, (jb, qt, spans, finish, ahead) in enumerate(items):
            if ahead is not None:
                ahead()
            top = score(rows_of(jb, qt), spans, bufs[n % 2], kv, kf, causal)
            if pending is not None:
                pending()
            pending = functools.partial(finish, jb, qt, spans, bufs[n % 2], top)
        pending()

    def begin(jb, qt, spans, buf, top):
        accs[jb, qt] = weigh(spans, buf, top, kv)
        tops[jb, qt] = top

    def merged(jb, qt, spans, buf, top):
        earlier = tops[jb, qt]
        both = jnp.maximum(earlier, top)
        factor = jnp.exp2(earlier - both)
        acc = accs[jb, qt] * jnp.concatenate([factor, factor], axis=1)
        return acc + weigh(spans, buf, both, kv), both

    def go_on(jb, qt, spans, buf, top):
        accs[jb, qt], tops[jb, qt] = merged(jb, qt, spans, buf, top)

    def close(jb, qt, spans, buf, top):
        give(jb, qt, merged(jb, qt, spans, buf, top)[0])

    def alone(jb, qt, spans, buf, top):
        give(jb, qt, weigh(spans, buf, top, kv))

    def wait_middle(jb):
        @pl.when(jb == 0)
        def _():
            stage_pair(2)
            stage_pair(3)

    def wait_last():
        @pl.when(takes(2))
        def _():
            for i in range(4):
                ctx_copy(2, i, SPAN).wait_recv()

    @pl.when(group > 0)
    def _():
        def early(jb, _):
            take_queries(jb)
            items = [(jb, qt, near(qt), begin, None) for qt in range(tiles_q)]
            for qt in range(tiles_q):
                ahead = functools.partial(wait_middle, jb) if qt == 0 else None
                items.append((jb, qt, MIDDLE, go_on, ahead))
            chain(items)
            return 0

        lax.fori_loop(0, groups, early, 0)
        wait_last()

        def late(jb, _):
            chain([(jb, qt, LAST, close, None) for qt in range(tiles_q)])
            return 0

        lax.fori_loop(0, groups, late, 0)

    @pl.when(group == 0)
    def _():
        stage_pair(2)
        stage_pair(3)

        def first(jb, _):
            take_queries(jb)
            chain([(jb, qt, near(qt)[:1], alone, None) for qt in range(tiles_q)])
            return 0

        lax.fori_loop(0, groups, first, 0)

    for i in range(1, 4):
        for which in range(2):
            kv_copy(which, i).wait_send()
        for j in range(HEADS):
            q_copy(j, i).wait_send()

    @pl.when(raw_out)
    def _():
        for i in (2, 3):
            for which in range(2):
                raw_copy(which, i).wait_send()

    for i in range(4):
        for d, sends in ((1, sends_right), (2, sends_pair), (3, sends_left), (4, sends_below(i))):
            @pl.when(sends)
            def _(d=d, i=i):
                ctx_copy(d, i, SPAN).wait_send()
    for jb in range(groups):
        for qt in range(tiles_q):
            out_copy(jb, qt).wait()


def shards(queries, keys, values, doc_lengths):
    anywhere = pl.BlockSpec(memory_space=pl.ANY)
    stacked = STACK * QROWS
    items = (HEADS // STACK, BLOCK // QROWS)
    return pl.pallas_call(
        kernel,
        out_shape=jax.ShapeDtypeStruct((BLOCK, HEADS * HEAD_SIZE), BF16),
        in_specs=[pl.BlockSpec(memory_space=pltpu.VMEM), anywhere, anywhere, anywhere],
        out_specs=anywhere,
        scratch_shapes=[
            pltpu.VMEM((HEADS, BLOCK, HEAD_SIZE), BF16),
            pltpu.VMEM((2, WINDOW, HEAD_SIZE), BF16),
            pltpu.VMEM((WINDOW, HEAD_SIZE), BF16),
            pltpu.VMEM((BLOCK, HEAD_SIZE), BF16),
            pltpu.VMEM((BLOCK, HEADS * HEAD_SIZE), BF16),
            pltpu.VMEM((stacked, 2 * BLOCK), F32),
            pltpu.VMEM((stacked, 2 * BLOCK), F32),
            pltpu.VMEM((*items, stacked, 2 * HEAD_SIZE), F32),
            pltpu.VMEM((*items, stacked, HEAD_SIZE), F32),
            pltpu.SemaphoreType.DMA((2, 4)),
            pltpu.SemaphoreType.DMA((2, 4)),
            pltpu.SemaphoreType.DMA((HEADS, 4)),
            pltpu.SemaphoreType.DMA((HEADS, 4)),
            pltpu.SemaphoreType.DMA((SPAN, 4)),
            pltpu.SemaphoreType.DMA((SPAN, 4)),
            pltpu.SemaphoreType.DMA((2, 2)),
            pltpu.SemaphoreType.DMA(items),
        ],
        compiler_params=pltpu.CompilerParams(
            collective_id=0, has_side_effects=True, vmem_limit_bytes=56 * 2**20
        ),
    )(doc_lengths.reshape(1, -1), queries, keys, values)


def solution(mesh):
    placed = (P(("ctx", "head"), None), P(("ctx", "head"), None), P(("ctx", "head"), None), P())
    return jax.shard_map(
        shards, mesh=mesh, in_specs=placed, out_specs=P("ctx", "head"), check_vma=False
    )
```

```python
import functools
import math

import jax
import jax.numpy as jnp
from jax import lax
from jax.experimental import pallas as pl
from jax.experimental.pallas import tpu as pltpu
from jax.sharding import PartitionSpec as P

QUERY_HEADS = 32
KEY_VALUE_HEADS = 4
HEAD_SIZE = 128
SPAN = 4
BLOCK = 512
CHUNK = 128
BACK = SPAN * BLOCK
WINDOW = BACK + BLOCK
PACKED = 65536
HEADS = QUERY_HEADS // KEY_VALUE_HEADS
SCALE = math.log2(math.e) / math.sqrt(HEAD_SIZE)
APART = -32768.0

MESH = pl.DeviceIdType.MESH
F32 = jnp.float32
BF16 = jnp.bfloat16

STACK = 4
QROWS = 128
BAND = BACK + QROWS


def nt(a, b):
    return lax.dot_general(a, b, (((1,), (1,)), ((), ())), preferred_element_type=F32)


def nn(a, b):
    return lax.dot_general(a, b, (((1,), (0,)), ((), ())), preferred_element_type=F32)


def partners(head):
    return [head, head + 1 - 2 * (head % 2), (head + 2) % 4, 3 - head]


def mark_documents(group, len_ref, kf, qf):
    lens = jnp.broadcast_to(len_ref[...], (16, 256))
    upto = (
        lax.broadcasted_iota(jnp.int32, (256, 256), 0)
        <= lax.broadcasted_iota(jnp.int32, (256, 256), 1)
    ).astype(F32).astype(BF16)
    high = (lens // 16).astype(F32).astype(BF16)
    low = (lens % 16).astype(F32).astype(BF16)
    ends = (nn(high, upto) * 16.0 + nn(low, upto))[0:1, :].astype(jnp.int32)
    ones = jnp.ones((256, 128), BF16)
    lane = lax.broadcasted_iota(jnp.int32, (512, 128), 1)
    for d in range(SPAN + 1):
        base = d * BLOCK
        pos = lax.broadcasted_iota(jnp.int32, (512, 256), 0) + (group * BLOCK + base + (PACKED - BACK)) % PACKED
        passed = jnp.where(ends <= pos, 1.0, 0.0).astype(BF16)
        index = nn(passed, ones).astype(jnp.int32)
        bit = jnp.right_shift(index, lane // 2) & 1
        differs = jnp.where(lane % 2 == 0, 1 - bit, bit)
        inside = lane < 16
        kf[base : base + BLOCK, :] = jnp.where(inside, differs.astype(F32) * APART, 0.0).astype(BF16)
        if d == SPAN:
            qf[...] = jnp.where(inside, (1 - differs).astype(F32), 0.0).astype(BF16)


def near(qt):
    return [(BACK, (qt + 1) * QROWS), (qt * QROWS, BLOCK - qt * QROWS)]


MIDDLE = [(3 * BLOCK, BLOCK), (BLOCK, BLOCK)]
LAST = [(2 * BLOCK, BLOCK)]


def score(q, spans, buf, kv, kf, causal):
    at, top = 0, None
    for lo, n in spans:
        k = jnp.concatenate([kv[0, lo : lo + n, :], kf[lo : lo + n, :]], axis=1)
        sc = nt(q, k)
        if lo == BACK:
            last = jnp.where(causal, sc[:, n - QROWS :], -1e30)
            sc = jnp.concatenate([sc[:, : n - QROWS], last], axis=1) if n > QROWS else last
        buf[:, at : at + n] = sc
        for a in range(0, n, 128):
            part = sc[:, a : a + 128]
            top = part if top is None else jnp.maximum(top, part)
        at += n
    return jnp.broadcast_to(jnp.max(top, axis=1, keepdims=True) * SCALE, top.shape)


def weigh(spans, buf, top, kv):
    at, acc = 0, None
    for lo, n in spans:
        shift = jnp.concatenate([top] * (n // 128), axis=1)
        p = jnp.exp2(buf[:, at : at + n] * SCALE - shift).astype(BF16)
        v = jnp.concatenate([kv[1, lo : lo + n, :], jnp.ones((n, 128), BF16)], axis=1)
        part = nn(p, v)
        acc = part if acc is None else acc + part
        at += n
    return acc


def kernel(
    len_ref, q_ref, k_ref, v_ref, o_ref,
    qbuf, kv, kf, qf, out, s0, s1, accs, tops,
    kv_send, kv_recv, q_send, q_recv, c_send, c_recv, raw_send, o_sem,
):
    group = lax.axis_index("ctx")
    head = lax.axis_index("head")
    x = group % 4
    row = group // 4
    below = (group + 4) % 128
    above = (group + 124) % 128
    right = row * 4 + (x + 1) % 4
    left = row * 4 + (x + 3) % 4
    pair = group + 1 - 2 * (x % 2)
    mates = partners(head)
    has_above = row > 0
    has_below = row < 31
    crosses = jnp.logical_and(row % 8 == 7, has_below)
    crossed = jnp.logical_and(row % 8 == 0, has_above)
    lower = head < 2

    barrier = pltpu.get_barrier_semaphore()

    def greet(who):
        pl.semaphore_signal(barrier, inc=1, device_id=who, device_id_type=MESH)

    for m in mates[1:]:
        greet((group, m))
    greet((right, head))
    greet((left, head))

    @pl.when(has_below)
    def _():
        greet((below, head))

    @pl.when(has_above)
    def _():
        greet((above, head))

    raw_out = jnp.logical_and(crosses, jnp.logical_not(lower))
    raw_in = jnp.logical_and(crossed, lower)

    @pl.when(raw_out)
    def _():
        greet((below, mates[2]))
        greet((below, mates[3]))

    @pl.when(raw_in)
    def _():
        greet((above, mates[2]))
        greet((above, mates[3]))

    greeters = 5 + has_below.astype(jnp.int32) + has_above.astype(jnp.int32)
    pl.semaphore_wait(barrier, greeters + 2 * jnp.logical_or(raw_out, raw_in).astype(jnp.int32))

    own = pl.ds(pl.multiple_of(head * CHUNK, CHUNK), CHUNK)
    own_kv = pl.ds(pl.multiple_of(BACK + head * CHUNK, CHUNK), CHUNK)

    def columns(start):
        return pl.ds(pl.multiple_of(start, 128), 128)

    def kv_copy(which, i):
        src = (k_ref, v_ref)[which].at[:, columns(mates[i] * 128)]
        dst = kv.at[which, own_kv, :]
        if i == 0:
            return pltpu.make_async_copy(src, dst, kv_recv.at[which, 0])
        return pltpu.make_async_remote_copy(
            src_ref=src, dst_ref=dst, send_sem=kv_send.at[which, i], recv_sem=kv_recv.at[which, i],
            device_id=(group, mates[i]), device_id_type=MESH,
        )

    def q_copy(j, i):
        src = q_ref.at[:, columns((mates[i] * HEADS + j) * 128)]
        dst = qbuf.at[j, own, :]
        if i == 0:
            return pltpu.make_async_copy(src, dst, q_recv.at[j, 0])
        return pltpu.make_async_remote_copy(
            src_ref=src, dst_ref=dst, send_sem=q_send.at[j, i], recv_sem=q_recv.at[j, i],
            device_id=(group, mates[i]), device_id_type=MESH,
        )

    def chunk(slot, i):
        return pl.ds(pl.multiple_of(slot * BLOCK + mates[i] * CHUNK, CHUNK), CHUNK)

    def ctx_copy(d, i, source):
        target = {1: right, 2: pair, 3: left, 4: below}[d]
        return pltpu.make_async_remote_copy(
            src_ref=kv.at[:, chunk(source, i), :], dst_ref=kv.at[:, chunk(SPAN - d, i), :],
            send_sem=c_send.at[d - 1, i], recv_sem=c_recv.at[d - 1, i],
            device_id=(target, head), device_id_type=MESH,
        )

    def raw_copy(which, i):
        src = (k_ref, v_ref)[which].at[:, columns(mates[i] * 128)]
        return pltpu.make_async_remote_copy(
            src_ref=src, dst_ref=kv.at[which, own, :],
            send_sem=raw_send.at[which, i - 2], recv_sem=c_recv.at[3, i],
            device_id=(below, mates[i]), device_id_type=MESH,
        )

    order = (2, 3, 1, 0)
    for i in order:
        for which in range(2):
            kv_copy(which, i).start()

    @pl.when(raw_out)
    def _():
        for i in (2, 3):
            for which in range(2):
                raw_copy(which, i).start()

    def send_queries(first, last, to):
        for j in range(first, last):
            for i in to:
                q_copy(j, i).start()

    yields = jnp.logical_and(crossed, lower)
    send_queries(0, STACK, order)

    @pl.when(jnp.logical_not(yields))
    def _():
        send_queries(STACK, HEADS, order)

    @pl.when(yields)
    def _():
        send_queries(STACK, HEADS, (1, 0))

    for d in range(1, SPAN + 1):
        @pl.when(group < d)
        def _(d=d):
            kv[:, (SPAN - d) * BLOCK : (SPAN - d + 1) * BLOCK, :] = jnp.zeros((2, BLOCK, HEAD_SIZE), BF16)

    mark_documents(group, len_ref, kf, qf)

    def sends_below(i):
        if i < 2:
            return has_below
        return jnp.logical_and(has_below, jnp.logical_not(jnp.logical_and(crosses, lower)))

    def takes(d):
        return group >= d

    own_right = x < 3
    own_left = x == 0
    up_right = jnp.logical_and(x == 3, has_above)
    up_left = jnp.logical_and(x > 0, has_above)
    sends_right = jnp.logical_or(own_right, up_right)
    sends_left = jnp.logical_or(own_left, up_left)
    sends_pair = jnp.logical_or(x >= 2, has_above)
    even = x % 2 == 0

    def stage_own(i):
        for which in range(2):
            if i == 0:
                kv_copy(which, i).wait()
            else:
                kv_copy(which, i).wait_recv()

        @pl.when(sends_below(i))
        def _():
            ctx_copy(4, i, SPAN).start()

        @pl.when(own_right)
        def _():
            ctx_copy(1, i, SPAN).start()

        @pl.when(own_left)
        def _():
            ctx_copy(3, i, SPAN).start()

    def stage_up(i):
        @pl.when(has_above)
        def _():
            ctx_copy(4, i, SPAN).wait_recv()

        @pl.when(up_right)
        def _():
            ctx_copy(1, i, 0).start()

        @pl.when(up_left)
        def _():
            ctx_copy(3, i, 0).start()

    def stage_pair(i):
        @pl.when(takes(1))
        def _():
            ctx_copy(1, i, SPAN).wait_recv()

        @pl.when(takes(3))
        def _():
            ctx_copy(3, i, SPAN).wait_recv()

        @pl.when(jnp.logical_and(sends_pair, even))
        def _():
            ctx_copy(2, i, SPAN - 1).start()

        @pl.when(jnp.logical_and(sends_pair, jnp.logical_not(even)))
        def _():
            ctx_copy(2, i, SPAN - 3).start()

    stage_own(0)
    stage_own(1)

    @pl.when(jnp.logical_not(crossed))
    def _():
        stage_up(0)

    stage_own(2)
    stage_own(3)

    @pl.when(crossed)
    def _():
        stage_up(0)

    stage_up(1)
    stage_up(2)
    stage_pair(0)
    stage_up(3)

    @pl.when(yields)
    def _():
        send_queries(STACK, HEADS, (2, 3))

    stage_pair(1)

    bufs = (s0, s1)
    tiles_q = BLOCK // QROWS
    groups = HEADS // STACK
    causal = lax.broadcasted_iota(jnp.int32, (QROWS, QROWS), 1) <= lax.broadcasted_iota(
        jnp.int32, (QROWS, QROWS), 0
    )
    causal = jnp.concatenate([causal] * STACK, axis=0)

    def rows_of(jb, qt):
        rows = slice(qt * QROWS, (qt + 1) * QROWS)
        marks = qf[rows, :]
        return jnp.concatenate(
            [jnp.concatenate([qbuf[jb * STACK + h, rows, :], marks], axis=1) for h in range(STACK)], axis=0
        )

    def out_copy(jb, qt):
        part = (pl.ds(qt * QROWS, QROWS), pl.ds(pl.multiple_of(jb * STACK * 128, 128), STACK * 128))
        return pltpu.make_async_copy(out.at[part], o_ref.at[part], o_sem.at[jb, qt])

    def take_queries(jb):
        for h in range(STACK):
            for i in range(4):
                if i == 0:
                    q_copy(jb * STACK + h, i).wait()
                else:
                    q_copy(jb * STACK + h, i).wait_recv()

    def give(jb, qt, acc):
        result = (acc[:, :128] / acc[:, 128:]).astype(BF16)
        for h in range(STACK):
            out[qt * QROWS : (qt + 1) * QROWS, columns((jb * STACK + h) * 128)] = result[
                h * QROWS : (h + 1) * QROWS
            ]
        out_copy(jb, qt).start()

    def chain(items):
        pending = None
        for n, (jb, qt, spans, finish, ahead) in enumerate(items):
            if ahead is not None:
                ahead()
            top = score(rows_of(jb, qt), spans, bufs[n % 2], kv, kf, causal)
            if pending is not None:
                pending()
            pending = functools.partial(finish, jb, qt, spans, bufs[n % 2], top)
        pending()

    def begin(jb, qt, spans, buf, top):
        accs[jb, qt] = weigh(spans, buf, top, kv)
        tops[jb, qt] = top

    def merged(jb, qt, spans, buf, top):
        earlier = tops[jb, qt]
        both = jnp.maximum(earlier, top)
        factor = jnp.exp2(earlier - both)
        acc = accs[jb, qt] * jnp.concatenate([factor, factor], axis=1)
        return acc + weigh(spans, buf, both, kv), both

    def go_on(jb, qt, spans, buf, top):
        accs[jb, qt], tops[jb, qt] = merged(jb, qt, spans, buf, top)

    def close(jb, qt, spans, buf, top):
        give(jb, qt, merged(jb, qt, spans, buf, top)[0])

    def alone(jb, qt, spans, buf, top):
        give(jb, qt, weigh(spans, buf, top, kv))

    def wait_middle(jb):
        @pl.when(jb == 0)
        def _():
            stage_pair(2)
            stage_pair(3)

    def wait_last():
        @pl.when(takes(2))
        def _():
            for i in range(4):
                ctx_copy(2, i, SPAN).wait_recv()

    @pl.when(group > 0)
    def _():
        def early(jb, _):
            take_queries(jb)
            items = [(jb, qt, near(qt), begin, None) for qt in range(tiles_q)]
            for qt in range(tiles_q):
                ahead = functools.partial(wait_middle, jb) if qt == 0 else None
                items.append((jb, qt, MIDDLE, go_on, ahead))
            chain(items)
            return 0

        lax.fori_loop(0, groups, early, 0)
        wait_last()

        def late(jb, _):
            chain([(jb, qt, LAST, close, None) for qt in range(tiles_q)])
            return 0

        lax.fori_loop(0, groups, late, 0)

    @pl.when(group == 0)
    def _():
        stage_pair(2)
        stage_pair(3)

        def first(jb, _):
            take_queries(jb)
            chain([(jb, qt, near(qt)[:1], alone, None) for qt in range(tiles_q)])
            return 0

        lax.fori_loop(0, groups, first, 0)

    for i in range(1, 4):
        for which in range(2):
            kv_copy(which, i).wait_send()
        for j in range(HEADS):
            q_copy(j, i).wait_send()

    @pl.when(raw_out)
    def _():
        for i in (2, 3):
            for which in range(2):
                raw_copy(which, i).wait_send()

    for i in range(4):
        for d, sends in ((1, sends_right), (2, sends_pair), (3, sends_left), (4, sends_below(i))):
            @pl.when(sends)
            def _(d=d, i=i):
                ctx_copy(d, i, SPAN).wait_send()
    for jb in range(groups):
        for qt in range(tiles_q):
            out_copy(jb, qt).wait()


def shards(queries, keys, values, doc_lengths):
    anywhere = pl.BlockSpec(memory_space=pl.ANY)
    stacked = STACK * QROWS
    items = (HEADS // STACK, BLOCK // QROWS)
    return pl.pallas_call(
        kernel,
        out_shape=jax.ShapeDtypeStruct((BLOCK, HEADS * HEAD_SIZE), BF16),
        in_specs=[pl.BlockSpec(memory_space=pltpu.VMEM), anywhere, anywhere, anywhere],
        out_specs=anywhere,
        scratch_shapes=[
            pltpu.VMEM((HEADS, BLOCK, HEAD_SIZE), BF16),
            pltpu.VMEM((2, WINDOW, HEAD_SIZE), BF16),
            pltpu.VMEM((WINDOW, HEAD_SIZE), BF16),
            pltpu.VMEM((BLOCK, HEAD_SIZE), BF16),
            pltpu.VMEM((BLOCK, HEADS * HEAD_SIZE), BF16),
            pltpu.VMEM((stacked, 2 * BLOCK), F32),
            pltpu.VMEM((stacked, 2 * BLOCK), F32),
            pltpu.VMEM((*items, stacked, 2 * HEAD_SIZE), F32),
            pltpu.VMEM((*items, stacked, HEAD_SIZE), F32),
            pltpu.SemaphoreType.DMA((2, 4)),
            pltpu.SemaphoreType.DMA((2, 4)),
            pltpu.SemaphoreType.DMA((HEADS, 4)),
            pltpu.SemaphoreType.DMA((HEADS, 4)),
            pltpu.SemaphoreType.DMA((SPAN, 4)),
            pltpu.SemaphoreType.DMA((SPAN, 4)),
            pltpu.SemaphoreType.DMA((2, 2)),
            pltpu.SemaphoreType.DMA(items),
        ],
        compiler_params=pltpu.CompilerParams(
            collective_id=0, has_side_effects=True, vmem_limit_bytes=56 * 2**20
        ),
    )(doc_lengths.reshape(1, -1), queries, keys, values)


def solution(mesh):
    placed = (P(("ctx", "head"), None), P(("ctx", "head"), None), P(("ctx", "head"), None), P())
    return jax.shard_map(
        shards, mesh=mesh, in_specs=placed, out_specs=P("ctx", "head"), check_vma=False
    )
```
